32 devices in a mesh: mem: 8 (over z, x), rep: 4 (over y, core).
Axes of the slice: x: 2, y: 2, z: 4, core: 2. Of those that a mesh axis runs over, the one named last changes fastest.
Arguments:
- states: bfloat16 [2048, 384], P('rep'), may hold values from -6 to 6
- batch_index: int32 [2, 2048], P(None, 'rep'), may hold values from 0 to 511
- obs_pick: int32 [2, 128], replicated, may hold values from 0 to 383
- norm_gain: float32 [384], replicated, may hold values from 0.5 to 1.5
- w_in: bfloat16 [384, 1024], replicated, may hold values from -0.3125 to 0.3125
- b_in: float32 [1024], replicated, may hold values from -0.5 to 0.5
- member_params: bfloat16 [8, 393216], P('mem', 'rep'), may hold values from -6 to 6
- observed: bfloat16 [2, 2048, 128], P(None, 'rep'), may hold values from -6 to 6
- perturbation: bfloat16 [8, 2, 2048, 128], P('mem', None, 'rep'), may hold values from -6 to 6
- inv_sigma: float32 [2, 2048, 128], P(None, 'rep'), may hold values from 0.5 to 4
Outputs:
- updated_params: bfloat16 [8, 393216], P('mem', 'rep')
The draws below stay inside these ranges and needn't reach their ends.
Inputs may be any that keep to these rules, and one draw needn't show every extreme that they name: `batch_index`: row number of a start state inside the block of 512 given states that belongs to its block of 512 batch rows. `obs_pick`: observed feature numbers; a number may repeat.
All inputs are finite; a program needn't handle non-finite values.
Results may differ from the reference program's by a relative error of at most 0.0056.
Values may be sent and summed in bfloat16 or wider, within the bound.
A program may use at most 64 MiB of HBM per device.

```python
import math
import jax
import jax.numpy as jnp
from jax import lax

S = 384
H = 1024
OBS_FEAT = 128
STEPS = 2
PASSES = 2
ROWS_DEV = 512
STATES_DEV = 512
MEMBERS = 8
BATCH = 2048
STATE_ROWS = 2048
PARAMS = 393216


def touch_ends(array, key, low, top_value):
    place = [jax.random.randint(jax.random.fold_in(key, axis), (), 0, length) for axis, length in enumerate(array.shape)]
    widest = array.shape.index(max(array.shape))
    neighbour = place[:widest] + [(place[widest] + 1) % array.shape[widest]] + place[widest + 1:]
    return array.at[tuple(place)].set(low).at[tuple(neighbour)].set(top_value)


def shard_levels(stream_key, extent, cuts, least, largest):
    level = 1.0
    for position, shards_of in cuts:
        draws = jax.random.uniform(jax.random.fold_in(jax.random.fold_in(stream_key, 6), position), (shards_of,), jnp.float32, least / len(cuts), largest / len(cuts))
        level = level * jnp.repeat(jnp.exp(draws), extent[position] // shards_of).reshape((-1,) + (1,) * (len(extent) - 1 - position))
    return level


def bell_draw(stream_key, shape, scale, bound, pieces=(), kind=jnp.bfloat16):
    result = scale * jax.random.normal(stream_key, shape, jnp.float32)
    if pieces:
        result = result * shard_levels(stream_key, shape, pieces, -0.22, 0.18)
    return jnp.clip(result, -bound, bound).astype(kind)


def setup_inputs(seed: int = 0) -> dict:
    seeds = jax.random.split(jax.random.key(seed), 11)
    states = bell_draw(seeds[0], (STATE_ROWS, S), 1.0, 6.0, ((0, 4),))
    batch_index = touch_ends(jax.random.randint(seeds[1], (STEPS, BATCH), 0, STATES_DEV), jax.random.fold_in(seeds[1], 1), 0, STATES_DEV - 1).astype(jnp.int32)
    obs_pick = touch_ends(jax.random.randint(seeds[2], (STEPS, OBS_FEAT), 0, S), jax.random.fold_in(seeds[2], 1), 0, S - 1).astype(jnp.int32)
    norm_gain = jnp.clip(1.0 + 0.1 * jax.random.normal(seeds[3], (S,), jnp.float32), 0.5, 1.5)
    w_in = bell_draw(seeds[4], (S, H), S ** -0.5, 0.3125)
    b_in = jnp.clip(jax.random.uniform(seeds[5], (H,), jnp.float32, -0.5, 0.5), -0.5, 0.5)
    member_params = bell_draw(seeds[6], (MEMBERS, PARAMS), 1.0, 6.0, ((0, 8), (1, 4)))
    observed = bell_draw(seeds[7], (STEPS, BATCH, OBS_FEAT), 1.0, 6.0, ((1, 4),))
    perturbation = bell_draw(seeds[8], (MEMBERS, STEPS, BATCH, OBS_FEAT), 1.0, 6.0, ((0, 8), (2, 4)))
    inv_sigma = jnp.clip(jnp.exp(math.log(4.0) - 2.0794415 * jax.random.uniform(seeds[9], (STEPS, BATCH, OBS_FEAT), jnp.float32) ** shard_levels(seeds[9], (STEPS, BATCH, OBS_FEAT), ((1, 4),), -0.2, 0.2)), 0.5, 4.0)
    return {"states": states, "batch_index": batch_index, "obs_pick": obs_pick, "norm_gain": norm_gain, "w_in": w_in, "b_in": b_in, "member_params": member_params, "observed": observed, "perturbation": perturbation, "inv_sigma": inv_sigma}


EPS = 1e-06
DT = 0.5

def hidden_layer(state, norm_gain, w_in, b_in):
    normed = (state * lax.rsqrt(lax.optimization_barrier(jnp.mean(state * state, axis=-1, keepdims=True)) + EPS) * norm_gain).astype(jnp.bfloat16)
    return jax.nn.gelu(jnp.dot(normed.astype(jnp.float32), w_in.astype(jnp.float32), preferred_element_type=jnp.float32) + b_in).astype(jnp.bfloat16)

def reference(states, batch_index, obs_pick, norm_gain, w_in, b_in, member_params, observed, perturbation, inv_sigma):
    block_base = jnp.arange(BATCH, dtype=jnp.int32) // ROWS_DEV * STATES_DEV
    row_numbers = (block_base[None, :] + batch_index).astype(jnp.int32)
    start_state = jnp.take(states, row_numbers, axis=0).astype(jnp.float32)
    shared = hidden_layer(start_state, norm_gain, w_in, b_in)
    step_scale = DT * H ** (-0.5)
    picks = jnp.broadcast_to(obs_pick[:, None, :], (STEPS, BATCH, OBS_FEAT)).astype(jnp.int32)

    def one_member(inputs):
        params, noise_row = inputs
        weights = params.reshape(H, S)
        current = start_state + step_scale * jnp.dot(shared.astype(jnp.float32), weights.astype(jnp.float32), preferred_element_type=jnp.float32)
        for pass_index in range(PASSES - 1):
            layer = hidden_layer(current, norm_gain, w_in, b_in)
            current = current + step_scale * jnp.dot(layer.astype(jnp.float32), weights.astype(jnp.float32), preferred_element_type=jnp.float32)
        predicted = jnp.take_along_axis(current, picks, axis=2)
        weighted = (predicted * inv_sigma).astype(jnp.bfloat16)
        misfit_w = (observed.astype(jnp.float32) * inv_sigma + noise_row.astype(jnp.float32) - predicted * inv_sigma).astype(jnp.bfloat16)
        return (weighted, misfit_w)
    weighted, misfit_w = lax.map(one_member, (member_params, perturbation))
    flat = weighted.reshape(MEMBERS, -1).astype(jnp.float32)
    anomaly = (flat - lax.optimization_barrier(jnp.mean(flat, axis=0))).astype(jnp.bfloat16)
    misfit_flat = misfit_w.reshape(MEMBERS, -1)
    gram_matrix = jnp.dot(anomaly.astype(jnp.float32), anomaly.T.astype(jnp.float32), preferred_element_type=jnp.float32)
    innovation = jnp.dot(anomaly.astype(jnp.float32), misfit_flat.T.astype(jnp.float32), preferred_element_type=jnp.float32)
    misfit = jnp.mean(jnp.square(misfit_flat.astype(jnp.float32)))
    system = gram_matrix + (1.0 + misfit) * (MEMBERS - 1) * jnp.eye(MEMBERS, dtype=jnp.float32)
    lower_factor = jnp.linalg.cholesky(system)
    halfway = lax.linalg.triangular_solve(lower_factor, innovation, left_side=True, lower=True)
    coefficients = lax.linalg.triangular_solve(lower_factor, halfway, left_side=True, lower=True, transpose_a=True)
    params_f = member_params.astype(jnp.float32)
    spread = params_f - lax.optimization_barrier(jnp.mean(params_f, axis=0))
    change = jnp.einsum('kj,kp->jp', coefficients, spread, precision=lax.Precision.HIGHEST)
    return (params_f + change).astype(jnp.bfloat16)
```

```python
import functools

import jax
import jax.numpy as jnp
from jax import lax
from jax.experimental import pallas as pl
from jax.experimental.pallas import tpu as pltpu
from jax.sharding import PartitionSpec as P

EPS = 1e-06
DT = 0.5
F32 = jnp.float32
BF16 = jnp.bfloat16
MESH = pl.DeviceIdType.MESH


def gelu(x):
    return 0.5 * x * (1.0 + jnp.tanh(0.7978845608028654 * (x + 0.044715 * (x * x * x))))


def dot(a, b):
    return jnp.dot(a, b, preferred_element_type=F32)


def halves(x):
    high = x.astype(BF16)
    low = (x - high.astype(F32)).astype(BF16)
    return jnp.concatenate([high, low], axis=1)


def kernel(
    members,
    entries,
    states_ref,
    index_ref,
    pick_ref,
    gain_ref,
    w_in_ref,
    b_in_ref,
    params_ref,
    observed_ref,
    noise_ref,
    sigma_ref,
    out_ref,
    w_buf,
    p_buf,
    e_send,
    e_buf,
    d_send,
    d_buf,
    g_send,
    g_buf,
    h_send,
    h_buf,
    new_buf,
    hid,
    w_sel,
    state_acc,
    pred_acc,
    start_sel,
    one_hot,
    weight_sum,
    anom,
    anom_w,
    resid,
    pairs,
    w_ssem,
    w_rsem,
    p_ssem,
    p_rsem,
    e_ssem,
    e_rsem,
    d_ssem,
    d_rsem,
    g_ssem,
    g_rsem,
    h_ssem,
    h_rsem,
    n_ssem,
    n_rsem,
):
    m = lax.axis_index("mem")
    r = lax.axis_index("rep")
    planes = members // 2
    z, x = m // 2, m % 2
    reps = w_buf.shape[0]
    rows, features = states_ref.shape
    steps, _ = index_ref.shape
    picked = pick_ref.shape[1]
    chunk = rows // members
    depth = params_ref.shape[0]
    width = w_in_ref.shape[1]
    block = depth // members
    scale = DT * width ** (-0.5)

    sibling = r + 1 - 2 * (r % 2)
    across = (r + 2) % reps
    diagonal = (sibling + 2) % reps

    far_first = sorted(range(planes), key=lambda d: -min(d, planes - d))
    steps_away = [(dz, dx) for dz in far_first for dx in range(2) if (dz, dx) != (0, 0)]

    def partner(dz, dx):
        return ((z + dz) % planes) * 2 + (x + dx) % 2

    def source(dz, dx):
        return ((z + planes - dz) % planes) * 2 + (x + 2 - dx) % 2

    barrier = pltpu.get_barrier_semaphore()
    for dz, dx in steps_away:
        pl.semaphore_signal(barrier, inc=1, device_id=(partner(dz, dx), r), device_id_type=MESH)
    for other in (sibling, across, diagonal):
        pl.semaphore_signal(barrier, inc=1, device_id=(m, other), device_id_type=MESH)
    pl.semaphore_wait(barrier, members - 1 + 3)

    def remote(src, dst, ssem, rsem, device):
        return pltpu.make_async_remote_copy(
            src_ref=src, dst_ref=dst, send_sem=ssem, recv_sem=rsem, device_id=device, device_id_type=MESH
        )

    to_across = remote(params_ref, w_buf.at[r], w_ssem.at[0], w_rsem.at[0], (m, across))
    to_sibling = remote(params_ref, w_buf.at[r], w_ssem.at[1], w_rsem.at[1], (m, sibling))
    relay = remote(w_buf.at[across], w_buf.at[across], w_ssem.at[2], w_rsem.at[2], (m, sibling))
    to_across.start()
    to_sibling.start()

    p_copies = []
    for dz, dx in steps_away:
        to, slot = partner(dz, dx), dz * 2 + dx
        copy = remote(
            params_ref.at[pl.ds(pl.multiple_of(to * block, block), block)],
            p_buf.at[m],
            p_ssem.at[slot],
            p_rsem.at[slot],
            (to, r),
        )
        copy.start()
        p_copies.append(copy)

    state_ids = lax.broadcasted_iota(jnp.int32, (rows, index_ref.shape[1]), 0)
    feature_ids = lax.broadcasted_iota(jnp.int32, (features, picked), 0)
    for k in range(steps):
        cols = slice(k * picked, (k + 1) * picked)
        hot = (state_ids == index_ref[k : k + 1, :]).astype(F32).astype(BF16)
        one_hot[k] = hot
        choose = (feature_ids == pick_ref[k : k + 1, :]).astype(F32).astype(BF16)
        start_sel[:, cols] = dot(states_ref[...], choose)
        sigma = sigma_ref[k]
        both = dot(hot, halves(sigma * sigma))
        total = both[:, :picked] + both[:, picked:]
        weight_sum[k] = total
        target = observed_ref[k].astype(F32) * sigma + noise_ref[k].astype(F32)
        both = dot(hot, halves(sigma * target))
        e_value = both[:, :picked] + both[:, picked:] - total * start_sel[:, cols]
        e_send[:, k] = e_value.astype(BF16).reshape(members, chunk, picked)

    e_copies = []
    for dz, dx in steps_away:
        to, slot = partner(dz, dx), dz * 2 + dx
        copy = remote(e_send.at[to], e_buf.at[m], e_ssem.at[slot], e_rsem.at[slot], (to, r))
        copy.start()
        e_copies.append(copy)
    e_buf[m] = e_send[m]

    gain = gain_ref[...]

    def normed(v):
        return (v * lax.rsqrt(jnp.mean(v * v, axis=-1, keepdims=True) + EPS) * gain).astype(BF16)

    first = normed(states_ref[...].astype(F32))
    for c in range(reps):
        cols = slice(c * depth, (c + 1) * depth)
        hid[c] = gelu(dot(first, w_in_ref[:, cols]) + b_in_ref[:, cols]).astype(BF16)

    choose = jnp.concatenate(
        [(feature_ids == pick_ref[k : k + 1, :]).astype(F32).astype(BF16) for k in range(steps)], axis=1
    )

    def use_shard(owner, shard, opening):
        layer = hid[owner]
        chosen = dot(shard, choose).astype(BF16)
        w_sel[owner] = chosen
        if opening:
            state_acc[...] = dot(layer, shard)
            pred_acc[...] = dot(layer, chosen)
        else:
            state_acc[...] += dot(layer, shard)
            pred_acc[...] += dot(layer, chosen)

    use_shard(r, params_ref[...], True)
    to_sibling.wait_recv()
    use_shard(sibling, w_buf[sibling], False)
    to_across.wait_recv()
    relay.start()
    use_shard(across, w_buf[across], False)
    relay.wait_recv()
    use_shard(diagonal, w_buf[diagonal], False)

    d_copies = []
    part = 2 * chunk
    for dz in far_first:
        plane = (z + dz) % planes
        at = pl.ds(pl.multiple_of(plane * part, part), part)
        current = states_ref[at, :].astype(F32) + scale * state_acc[at, :]
        second = normed(current)
        total = pred_acc[at, :]
        for c in range(reps):
            cols = slice(c * depth, (c + 1) * depth)
            layer = gelu(dot(second, w_in_ref[:, cols]) + b_in_ref[:, cols]).astype(BF16)
            total += dot(layer, w_sel[c])
        delta = scale * total
        pred_acc[at, :] = delta
        for k in range(steps):
            value = delta[:, k * picked : (k + 1) * picked].astype(BF16)
            d_send[pl.ds(plane * 2, 2), k] = value.reshape(2, chunk, picked)
        for dx in range(2):
            if (dz, dx) != (0, 0):
                to, slot = plane * 2 + (x + dx) % 2, dz * 2 + dx
                copy = remote(d_send.at[to], d_buf.at[m], d_ssem.at[slot], d_rsem.at[slot], (to, r))
                copy.start()
                d_copies.append(copy)
    d_buf[m] = d_send[m]

    squares = jnp.zeros((index_ref.shape[1], picked), F32)
    for k in range(steps):
        cols = slice(k * picked, (k + 1) * picked)
        both = lax.dot_general(
            one_hot[k],
            halves(start_sel[:, cols] + pred_acc[:, cols]),
            (((0,), (0,)), ((), ())),
            preferred_element_type=F32,
        )
        predicted = both[:, :picked] + both[:, picked:]
        sigma = sigma_ref[k]
        miss = observed_ref[k].astype(F32) * sigma + noise_ref[k].astype(F32) - predicted * sigma
        squares += miss * miss
    misfit_local = jnp.sum(jnp.sum(squares, axis=0, keepdims=True), axis=1, keepdims=True)

    mine = pl.ds(pl.multiple_of(m * chunk, chunk), chunk)
    d_weight = weight_sum[:, mine, :]

    for copy in e_copies:
        copy.wait_recv()
    for copy in d_copies:
        copy.wait_recv()

    mean = d_buf[0].astype(F32)
    for j in range(1, members):
        mean += d_buf[j].astype(F32)
    mean = mean * (1.0 / members)
    for j in range(members):
        value = d_buf[j].astype(F32)
        anom[j] = value - mean
        anom_w[j] = (value - mean) * d_weight
        resid[j] = e_buf[j].astype(F32) - value * d_weight
    slabs = steps * chunk // 8
    for j in range(members):
        left = anom[j].reshape(slabs, 8, picked)
        for l in range(members):
            right = anom_w[l].reshape(slabs, 8, picked)
            pairs[pl.ds((l * members + j) * 8, 8), :] = jnp.sum(left * right, axis=0)
            right = resid[l].reshape(slabs, 8, picked)
            pairs[pl.ds(((members + l) * members + j) * 8, 8), :] = jnp.sum(left * right, axis=0)
    count = 2 * members * members
    sums = pairs[pl.ds(0, count, stride=8), :]
    for s in range(1, 8):
        sums += pairs[pl.ds(s, count, stride=8), :]
    sums = jnp.sum(sums, axis=1, keepdims=True)
    lanes = lax.broadcasted_iota(jnp.int32, (members, 128), 1)
    packed = jnp.where(lanes == 2 * members, misfit_local, 0.0)
    for l in range(2 * members):
        packed = jnp.where(lanes == l, sums[l * members : (l + 1) * members, :], packed)
    g_send[...] = packed
    g_buf[m] = packed

    g_copies = []
    for dz, dx in steps_away:
        to, slot = partner(dz, dx), dz * 2 + dx
        copy = remote(g_send, g_buf.at[m], g_ssem.at[slot], g_rsem.at[slot], (to, r))
        copy.start()
        g_copies.append(copy)
    for copy in g_copies:
        copy.wait_recv()
    total = g_buf[0]
    for j in range(1, members):
        total += g_buf[j]
    h_send[...] = total
    h_buf[r] = total
    h_copies = []
    for slot, other in enumerate((sibling, across, diagonal)):
        copy = remote(h_send, h_buf.at[r], h_ssem.at[slot], h_rsem.at[slot], (m, other))
        copy.start()
        h_copies.append(copy)
    for copy in h_copies:
        copy.wait_recv()
    total = h_buf[0]
    for j in range(1, reps):
        total += h_buf[j]

    row_ids = lax.broadcasted_iota(jnp.int32, (members, 128), 0)
    misfit = total[:, 2 * members : 2 * members + 1] * (1.0 / entries)
    table = total + jnp.where(row_ids == lanes, (1.0 + misfit) * (members - 1), 0.0)
    for j in range(members):
        row = table[j : j + 1, :] / table[j : j + 1, j : j + 1]
        table = jnp.where(row_ids == j, row, table - table[:, j : j + 1] * row)
    centred = table - jnp.sum(table, axis=0, keepdims=True) * (1.0 / members)

    for copy in p_copies:
        copy.wait_recv()
    p_buf[m] = params_ref[pl.ds(pl.multiple_of(m * block, block), block), :]
    values = [p_buf[k].astype(F32) for k in range(members)]
    for j in range(members):
        change = values[0] * centred[0:1, members + j : members + j + 1]
        for k in range(1, members):
            change += values[k] * centred[k : k + 1, members + j : members + j + 1]
        new_buf[j] = (values[j] + change).astype(BF16)
    n_copies = []
    here = pl.ds(pl.multiple_of(m * block, block), block)
    for dz, dx in steps_away:
        to, slot = partner(dz, dx), dz * 2 + dx
        copy = remote(new_buf.at[to], out_ref.at[here], n_ssem.at[slot], n_rsem.at[slot], (to, r))
        copy.start()
        n_copies.append(copy)
    out_ref[here, :] = new_buf[m]
    for dz, dx in steps_away:
        slot = dz * 2 + dx
        came = source(dz, dx)
        remote(
            new_buf.at[came],
            out_ref.at[pl.ds(pl.multiple_of(came * block, block), block)],
            n_ssem.at[slot],
            n_rsem.at[slot],
            (came, r),
        ).wait_recv()
    for copy in [to_across, to_sibling, relay] + p_copies + e_copies + d_copies + g_copies + h_copies + n_copies:
        copy.wait_send()


def fused(members, reps, entries, *args):
    states, batch_index, obs_pick, norm_gain, w_in, b_in, params, observed, noise, sigma = args
    rows, features = states.shape
    width = w_in.shape[1]
    steps, picked = obs_pick.shape
    depth = width // reps
    chunk = rows // members
    block = depth // members
    piece = (members, steps, chunk, picked)
    dma = pltpu.SemaphoreType.DMA
    vmem = pl.BlockSpec(memory_space=pltpu.VMEM)
    scratch = [
        pltpu.VMEM((reps, depth, features), BF16),
        pltpu.VMEM((members, block, features), BF16),
        pltpu.VMEM(piece, BF16),
        pltpu.VMEM(piece, BF16),
        pltpu.VMEM(piece, BF16),
        pltpu.VMEM(piece, BF16),
        pltpu.VMEM((members, 128), F32),
        pltpu.VMEM((members, members, 128), F32),
        pltpu.VMEM((members, 128), F32),
        pltpu.VMEM((reps, members, 128), F32),
        pltpu.VMEM((members, block, features), BF16),
        pltpu.VMEM((reps, rows, depth), BF16),
        pltpu.VMEM((reps, depth, steps * picked), BF16),
        pltpu.VMEM((rows, features), F32),
        pltpu.VMEM((rows, steps * picked), F32),
        pltpu.VMEM((rows, steps * picked), F32),
        pltpu.VMEM((steps, rows, batch_index.shape[1]), BF16),
        pltpu.VMEM((steps, rows, picked), F32),
        pltpu.VMEM(piece, F32),
        pltpu.VMEM(piece, F32),
        pltpu.VMEM(piece, F32),
        pltpu.VMEM((2 * members * members * 8, picked), F32),
        dma((3,)),
        dma((3,)),
    ]
    for count in (members, members, members, members, 3, members):
        scratch += [dma((count,)), dma((count,))]
    return pl.pallas_call(
        functools.partial(kernel, members, entries),
        out_shape=jax.ShapeDtypeStruct((depth, features), BF16),
        in_specs=[vmem] * 10,
        out_specs=vmem,
        scratch_shapes=scratch,
        compiler_params=pltpu.CompilerParams(
            collective_id=0, has_side_effects=True, vmem_limit_bytes=48 * 1024 * 1024
        ),
        cost_estimate=pl.CostEstimate(flops=4 * 10**9, bytes_accessed=4 * 10**6, transcendentals=10**6),
    )(
        states,
        batch_index,
        obs_pick,
        norm_gain.reshape(1, features),
        w_in,
        b_in.reshape(1, width),
        params.reshape(depth, features),
        observed,
        noise.reshape(noise.shape[1:]),
        sigma,
    ).reshape(params.shape)


def hidden_layer(state, norm_gain, w_in, b_in):
    normed = (
        state * lax.rsqrt(jnp.mean(state * state, axis=-1, keepdims=True) + EPS) * norm_gain
    ).astype(jnp.bfloat16)
    return jax.nn.gelu(jnp.dot(normed, w_in, preferred_element_type=jnp.float32) + b_in).astype(
        jnp.bfloat16
    )


def member_sums(pieces):
    weighted, misfit_w = pieces
    count = weighted.shape[0]
    gram_list = []
    innov_list = []
    for item_index in range(weighted.shape[1]):
        flat = weighted[:, item_index].reshape(count, -1).astype(jnp.float32)
        anomaly = (flat - jnp.mean(flat, axis=0)).astype(jnp.bfloat16)
        misfit_flat = misfit_w[:, item_index].reshape(count, -1)
        gram_list.append(
            lax.dot_general(
                anomaly, anomaly, (((1,), (1,)), ((), ())), preferred_element_type=jnp.float32
            )
        )
        innov_list.append(
            lax.dot_general(
                anomaly, misfit_flat, (((1,), (1,)), ((), ())), preferred_element_type=jnp.float32
            )
        )
    return (jnp.stack(gram_list, axis=0), jnp.stack(innov_list, axis=0))


def solve_columns(system, right_side):
    lower_factor = jnp.linalg.cholesky(system)
    halfway = lax.linalg.triangular_solve(lower_factor, right_side, left_side=True, lower=True)
    return lax.linalg.triangular_solve(
        lower_factor, halfway, left_side=True, lower=True, transpose_a=True
    )


def spread_out(
    states,
    batch_index,
    obs_pick,
    norm_gain,
    w_in,
    b_in,
    member_params,
    observed,
    perturbation,
    inv_sigma,
):
    local_members = member_params.shape[0]
    width = w_in.shape[1]
    features = w_in.shape[0]
    step_count = batch_index.shape[0]
    picked = obs_pick.shape[1]
    whole_params = lax.all_gather(member_params, "rep", axis=1, tiled=True)
    weights = whole_params.reshape(local_members, width, features)
    step_scale = DT * width ** (-0.5)
    start_state = jnp.take(states, batch_index, axis=0).astype(jnp.float32)
    shared = hidden_layer(start_state, norm_gain, w_in, b_in)
    current = start_state[None] + step_scale * jnp.einsum(
        "kbh,jhs->jkbs", shared, weights, preferred_element_type=jnp.float32
    )
    layer = hidden_layer(current, norm_gain, w_in, b_in)
    current = current + step_scale * jnp.einsum(
        "jkbh,jhs->jkbs", layer, weights, preferred_element_type=jnp.float32
    )
    feature_ids = lax.broadcasted_iota(jnp.int32, (step_count, features, picked), 1)
    selector = (feature_ids == obs_pick[:, None, :]).astype(jnp.float32)
    predicted = jnp.einsum("jkbs,ksf->jkbf", current, selector, precision=lax.Precision.HIGHEST)
    weighted = (predicted * inv_sigma).astype(jnp.bfloat16)
    misfit_w = (
        observed.astype(jnp.float32) * inv_sigma
        + perturbation.astype(jnp.float32)
        - predicted * inv_sigma
    ).astype(jnp.bfloat16)
    misfit_local = jnp.sum(jnp.square(misfit_w.astype(jnp.float32)))
    gram_items, innov_items = member_sums(
        (
            lax.all_to_all(weighted, "mem", split_axis=2, concat_axis=0, tiled=True),
            lax.all_to_all(misfit_w, "mem", split_axis=2, concat_axis=0, tiled=True),
        )
    )
    gram_matrix = jnp.sum(gram_items, axis=0)
    innovation = jnp.sum(innov_items, axis=0)
    members = gram_matrix.shape[0]
    entries = members * step_count * batch_index.shape[1] * lax.axis_size("rep") * picked
    identity = jnp.eye(members, dtype=jnp.float32)
    gram_matrix, innovation, misfit_total = lax.psum(
        (gram_matrix, innovation, misfit_local), ("mem", "rep")
    )
    system = gram_matrix + (1.0 + misfit_total / entries) * (members - 1) * identity
    coefficients = solve_columns(system, innovation)
    param_block = lax.all_to_all(member_params, "mem", split_axis=1, concat_axis=0, tiled=True)
    params_f = param_block.astype(jnp.float32)
    spread = params_f - jnp.mean(params_f, axis=0)
    change = jnp.einsum("kj,kp->jp", coefficients, spread, precision=lax.Precision.HIGHEST)
    renewed = (params_f + change).astype(jnp.bfloat16)
    return lax.all_to_all(renewed, "mem", split_axis=0, concat_axis=1, tiled=True)


def on_device(states, batch_index, obs_pick, norm_gain, w_in, b_in, member_params, observed, perturbation, inv_sigma):
    args = (states, batch_index, obs_pick, norm_gain, w_in, b_in, member_params, observed, perturbation, inv_sigma)
    members, reps = lax.axis_size("mem"), lax.axis_size("rep")
    if members <= 8 and reps == 4 and member_params.shape[0] == 1:
        entries = members * batch_index.size * reps * obs_pick.shape[1]
        return fused(members, reps, entries, *args)
    return spread_out(*args)


def solution(mesh):
    placed = (
        P("rep", None),
        P(None, "rep"),
        P(),
        P(),
        P(),
        P(),
        P("mem", "rep"),
        P(None, "rep", None),
        P("mem", None, "rep", None),
        P(None, "rep", None),
    )
    return jax.shard_map(
        on_device, mesh=mesh, in_specs=placed, out_specs=P("mem", "rep"), check_vma=False
    )
```

```python
import functools

import jax
import jax.numpy as jnp
from jax import lax
from jax.experimental import pallas as pl
from jax.experimental.pallas import tpu as pltpu
from jax.sharding import PartitionSpec as P

EPS = 1e-06
DT = 0.5
F32 = jnp.float32
BF16 = jnp.bfloat16
MESH = pl.DeviceIdType.MESH


def gelu(x):
    return 0.5 * x * (1.0 + jnp.tanh(0.7978845608028654 * (x + 0.044715 * (x * x * x))))


def dot(a, b):
    return jnp.dot(a, b, preferred_element_type=F32)


def halves(x):
    high = x.astype(BF16)
    low = (x - high.astype(F32)).astype(BF16)
    return jnp.concatenate([high, low], axis=1)


def kernel(
    members,
    entries,
    states_hbm,
    index_hbm,
    pick_hbm,
    gain_hbm,
    w_in_hbm,
    b_in_hbm,
    params_hbm,
    observed_hbm,
    noise_hbm,
    sigma_hbm,
    out_ref,
    w_buf,
    p_buf,
    e_send,
    e_buf,
    d_send,
    d_buf,
    g_send,
    g_buf,
    h_send,
    h_buf,
    new_buf,
    hid,
    w_sel,
    state_acc,
    pred_acc,
    start_sel,
    one_hot,
    weight_sum,
    anom,
    anom_w,
    resid,
    pairs,
    w_ssem,
    w_rsem,
    p_ssem,
    p_rsem,
    e_ssem,
    e_rsem,
    d_ssem,
    d_rsem,
    g_ssem,
    g_rsem,
    h_ssem,
    h_rsem,
    n_ssem,
    n_rsem,
    states_ref,
    index_ref,
    pick_ref,
    gain_ref,
    w_in_ref,
    b_in_ref,
    params_ref,
    observed_ref,
    noise_ref,
    sigma_ref,
    raw,
    in_sem,
):
    m = lax.axis_index("mem")
    r = lax.axis_index("rep")
    planes = members // 2
    z, x = m // 2, m % 2
    reps = w_buf.shape[0]
    rows, features = states_ref.shape
    steps, _ = index_ref.shape
    picked = pick_ref.shape[1]
    chunk = rows // members
    depth = params_ref.shape[0]
    width = w_in_ref.shape[1]
    block = depth // members
    scale = DT * width ** (-0.5)

    sibling = r + 1 - 2 * (r % 2)
    across = (r + 2) % reps
    diagonal = (sibling + 2) % reps

    far_first = sorted(range(planes), key=lambda d: -min(d, planes - d))
    steps_away = [(dz, dx) for dz in far_first for dx in range(2) if (dz, dx) != (0, 0)]

    def partner(dz, dx):
        return ((z + dz) % planes) * 2 + (x + dx) % 2

    def source(dz, dx):
        return ((z + planes - dz) % planes) * 2 + (x + 2 - dx) % 2

    barrier = pltpu.get_barrier_semaphore()
    for dz, dx in steps_away:
        pl.semaphore_signal(barrier, inc=1, device_id=(partner(dz, dx), r), device_id_type=MESH)
    for other in (sibling, across, diagonal):
        pl.semaphore_signal(barrier, inc=1, device_id=(m, other), device_id_type=MESH)

    def load(slot, src, dst):
        copy = pltpu.make_async_copy(src, dst, in_sem.at[slot])
        copy.start()
        return copy

    get_params = load(6, params_hbm, raw)
    get_index = load(1, index_hbm, index_ref)
    get_pick = load(2, pick_hbm, pick_ref)
    get_states = load(0, states_hbm, states_ref)
    get_sigma = load(9, sigma_hbm, sigma_ref)
    get_observed = load(7, observed_hbm, observed_ref)
    get_noise = load(8, noise_hbm, noise_ref)
    get_gain = load(3, gain_hbm, gain_ref)
    get_b_in = load(5, b_in_hbm, b_in_ref)
    get_w_in = load(4, w_in_hbm, w_in_ref)
    get_params.wait()
    params_ref[...] = raw[...].reshape(depth, features)
    pl.semaphore_wait(barrier, members - 1 + 3)

    def remote(src, dst, ssem, rsem, device):
        return pltpu.make_async_remote_copy(
            src_ref=src, dst_ref=dst, send_sem=ssem, recv_sem=rsem, device_id=device, device_id_type=MESH
        )

    to_across = remote(params_ref, w_buf.at[r], w_ssem.at[0], w_rsem.at[0], (m, across))
    to_sibling = remote(params_ref, w_buf.at[r], w_ssem.at[1], w_rsem.at[1], (m, sibling))
    relay = remote(w_buf.at[across], w_buf.at[across], w_ssem.at[2], w_rsem.at[2], (m, sibling))
    to_across.start()
    to_sibling.start()

    p_copies = []
    for dz, dx in steps_away:
        to, slot = partner(dz, dx), dz * 2 + dx
        copy = remote(
            params_ref.at[pl.ds(pl.multiple_of(to * block, block), block)],
            p_buf.at[m],
            p_ssem.at[slot],
            p_rsem.at[slot],
            (to, r),
        )
        copy.start()
        p_copies.append(copy)

    get_index.wait()
    get_pick.wait()
    get_states.wait()
    get_sigma.wait()
    get_observed.wait()
    get_noise.wait()

    state_ids = lax.broadcasted_iota(jnp.int32, (rows, index_ref.shape[1]), 0)
    feature_ids = lax.broadcasted_iota(jnp.int32, (features, picked), 0)
    for k in range(steps):
        cols = slice(k * picked, (k + 1) * picked)
        hot = (state_ids == index_ref[k : k + 1, :]).astype(F32).astype(BF16)
        one_hot[k] = hot
        choose = (feature_ids == pick_ref[k : k + 1, :]).astype(F32).astype(BF16)
        start_sel[:, cols] = dot(states_ref[...], choose)
        sigma = sigma_ref[k]
        both = dot(hot, halves(sigma * sigma))
        total = both[:, :picked] + both[:, picked:]
        weight_sum[k] = total
        target = observed_ref[k].astype(F32) * sigma + noise_ref[k].astype(F32)
        both = dot(hot, halves(sigma * target))
        e_value = both[:, :picked] + both[:, picked:] - total * start_sel[:, cols]
        e_send[:, k] = e_value.astype(BF16).reshape(members, chunk, picked)

    e_copies = []
    for dz, dx in steps_away:
        to, slot = partner(dz, dx), dz * 2 + dx
        copy = remote(e_send.at[to], e_buf.at[m], e_ssem.at[slot], e_rsem.at[slot], (to, r))
        copy.start()
        e_copies.append(copy)
    e_buf[m] = e_send[m]

    get_gain.wait()
    get_b_in.wait()
    get_w_in.wait()
    gain = gain_ref[...].reshape(1, features)

    def normed(v):
        return (v * lax.rsqrt(jnp.mean(v * v, axis=-1, keepdims=True) + EPS) * gain).astype(BF16)

    first = normed(states_ref[...].astype(F32))
    for c in range(reps):
        cols = slice(c * depth, (c + 1) * depth)
        hid[c] = gelu(dot(first, w_in_ref[:, cols]) + b_in_ref[:, cols]).astype(BF16)

    choose = jnp.concatenate(
        [(feature_ids == pick_ref[k : k + 1, :]).astype(F32).astype(BF16) for k in range(steps)], axis=1
    )

    def use_shard(owner, shard, opening):
        layer = hid[owner]
        chosen = dot(shard, choose).astype(BF16)
        w_sel[owner] = chosen
        if opening:
            state_acc[...] = dot(layer, shard)
            pred_acc[...] = dot(layer, chosen)
        else:
            state_acc[...] += dot(layer, shard)
            pred_acc[...] += dot(layer, chosen)

    use_shard(r, params_ref[...], True)
    to_sibling.wait_recv()
    use_shard(sibling, w_buf[sibling], False)
    to_across.wait_recv()
    relay.start()
    use_shard(across, w_buf[across], False)
    relay.wait_recv()
    use_shard(diagonal, w_buf[diagonal], False)

    d_copies = []
    part = 2 * chunk
    for dz in far_first:
        plane = (z + dz) % planes
        at = pl.ds(pl.multiple_of(plane * part, part), part)
        current = states_ref[at, :].astype(F32) + scale * state_acc[at, :]
        second = normed(current)
        total = pred_acc[at, :]
        for c in range(reps):
            cols = slice(c * depth, (c + 1) * depth)
            layer = gelu(dot(second, w_in_ref[:, cols]) + b_in_ref[:, cols]).astype(BF16)
            total += dot(layer, w_sel[c])
        delta = scale * total
        pred_acc[at, :] = delta
        for k in range(steps):
            value = delta[:, k * picked : (k + 1) * picked].astype(BF16)
            d_send[pl.ds(plane * 2, 2), k] = value.reshape(2, chunk, picked)
        for dx in range(2):
            if (dz, dx) != (0, 0):
                to, slot = plane * 2 + (x + dx) % 2, dz * 2 + dx
                copy = remote(d_send.at[to], d_buf.at[m], d_ssem.at[slot], d_rsem.at[slot], (to, r))
                copy.start()
                d_copies.append(copy)
    d_buf[m] = d_send[m]

    squares = jnp.zeros((index_ref.shape[1], picked), F32)
    for k in range(steps):
        cols = slice(k * picked, (k + 1) * picked)
        both = lax.dot_general(
            one_hot[k],
            halves(start_sel[:, cols] + pred_acc[:, cols]),
            (((0,), (0,)), ((), ())),
            preferred_element_type=F32,
        )
        predicted = both[:, :picked] + both[:, picked:]
        sigma = sigma_ref[k]
        miss = observed_ref[k].astype(F32) * sigma + noise_ref[k].astype(F32) - predicted * sigma
        squares += miss * miss
    misfit_local = jnp.sum(jnp.sum(squares, axis=0, keepdims=True), axis=1, keepdims=True)

    mine = pl.ds(pl.multiple_of(m * chunk, chunk), chunk)
    d_weight = weight_sum[:, mine, :]

    for copy in e_copies:
        copy.wait_recv()
    for copy in d_copies:
        copy.wait_recv()

    mean = d_buf[0].astype(F32)
    for j in range(1, members):
        mean += d_buf[j].astype(F32)
    mean = mean * (1.0 / members)
    for j in range(members):
        value = d_buf[j].astype(F32)
        anom[j] = value - mean
        anom_w[j] = (value - mean) * d_weight
        resid[j] = e_buf[j].astype(F32) - value * d_weight
    slabs = steps * chunk // 8
    for j in range(members):
        left = anom[j].reshape(slabs, 8, picked)
        for l in range(members):
            right = anom_w[l].reshape(slabs, 8, picked)
            pairs[pl.ds((l * members + j) * 8, 8), :] = jnp.sum(left * right, axis=0)
            right = resid[l].reshape(slabs, 8, picked)
            pairs[pl.ds(((members + l) * members + j) * 8, 8), :] = jnp.sum(left * right, axis=0)
    count = 2 * members * members
    sums = pairs[pl.ds(0, count, stride=8), :]
    for s in range(1, 8):
        sums += pairs[pl.ds(s, count, stride=8), :]
    sums = jnp.sum(sums, axis=1, keepdims=True)
    lanes = lax.broadcasted_iota(jnp.int32, (members, 128), 1)
    packed = jnp.where(lanes == 2 * members, misfit_local, 0.0)
    for l in range(2 * members):
        packed = jnp.where(lanes == l, sums[l * members : (l + 1) * members, :], packed)
    g_send[...] = packed
    g_buf[m] = packed

    g_copies = []
    for dz, dx in steps_away:
        to, slot = partner(dz, dx), dz * 2 + dx
        copy = remote(g_send, g_buf.at[m], g_ssem.at[slot], g_rsem.at[slot], (to, r))
        copy.start()
        g_copies.append(copy)
    for copy in g_copies:
        copy.wait_recv()
    total = g_buf[0]
    for j in range(1, members):
        total += g_buf[j]
    h_send[...] = total
    h_buf[r] = total
    h_copies = []
    for slot, other in enumerate((sibling, across, diagonal)):
        copy = remote(h_send, h_buf.at[r], h_ssem.at[slot], h_rsem.at[slot], (m, other))
        copy.start()
        h_copies.append(copy)
    for copy in h_copies:
        copy.wait_recv()
    total = h_buf[0]
    for j in range(1, reps):
        total += h_buf[j]

    row_ids = lax.broadcasted_iota(jnp.int32, (members, 128), 0)
    misfit = total[:, 2 * members : 2 * members + 1] * (1.0 / entries)
    table = total + jnp.where(row_ids == lanes, (1.0 + misfit) * (members - 1), 0.0)
    for j in range(members):
        row = table[j : j + 1, :] / table[j : j + 1, j : j + 1]
        table = jnp.where(row_ids == j, row, table - table[:, j : j + 1] * row)
    centred = table - jnp.sum(table, axis=0, keepdims=True) * (1.0 / members)

    for copy in p_copies:
        copy.wait_recv()
    p_buf[m] = params_ref[pl.ds(pl.multiple_of(m * block, block), block), :]
    values = [p_buf[k].astype(F32) for k in range(members)]
    for j in range(members):
        change = values[0] * centred[0:1, members + j : members + j + 1]
        for k in range(1, members):
            change += values[k] * centred[k : k + 1, members + j : members + j + 1]
        new_buf[j] = (values[j] + change).astype(BF16)
    n_copies = []
    here = pl.ds(pl.multiple_of(m * block, block), block)
    for dz, dx in steps_away:
        to, slot = partner(dz, dx), dz * 2 + dx
        copy = remote(new_buf.at[to], out_ref.at[here], n_ssem.at[slot], n_rsem.at[slot], (to, r))
        copy.start()
        n_copies.append(copy)
    out_ref[here, :] = new_buf[m]
    for dz, dx in steps_away:
        slot = dz * 2 + dx
        came = source(dz, dx)
        remote(
            new_buf.at[came],
            out_ref.at[pl.ds(pl.multiple_of(came * block, block), block)],
            n_ssem.at[slot],
            n_rsem.at[slot],
            (came, r),
        ).wait_recv()
    for copy in [to_across, to_sibling, relay] + p_copies + e_copies + d_copies + g_copies + h_copies + n_copies:
        copy.wait_send()


def fused(members, reps, entries, *args):
    states, batch_index, obs_pick, norm_gain, w_in, b_in, params, observed, noise, sigma = args
    rows, features = states.shape
    width = w_in.shape[1]
    steps, picked = obs_pick.shape
    depth = width // reps
    chunk = rows // members
    block = depth // members
    piece = (members, steps, chunk, picked)
    dma = pltpu.SemaphoreType.DMA
    vmem = pl.BlockSpec(memory_space=pltpu.VMEM)
    hbm = pl.BlockSpec(memory_space=pltpu.HBM)
    scratch = [
        pltpu.VMEM((reps, depth, features), BF16),
        pltpu.VMEM((members, block, features), BF16),
        pltpu.VMEM(piece, BF16),
        pltpu.VMEM(piece, BF16),
        pltpu.VMEM(piece, BF16),
        pltpu.VMEM(piece, BF16),
        pltpu.VMEM((members, 128), F32),
        pltpu.VMEM((members, members, 128), F32),
        pltpu.VMEM((members, 128), F32),
        pltpu.VMEM((reps, members, 128), F32),
        pltpu.VMEM((members, block, features), BF16),
        pltpu.VMEM((reps, rows, depth), BF16),
        pltpu.VMEM((reps, depth, steps * picked), BF16),
        pltpu.VMEM((rows, features), F32),
        pltpu.VMEM((rows, steps * picked), F32),
        pltpu.VMEM((rows, steps * picked), F32),
        pltpu.VMEM((steps, rows, batch_index.shape[1]), BF16),
        pltpu.VMEM((steps, rows, picked), F32),
        pltpu.VMEM(piece, F32),
        pltpu.VMEM(piece, F32),
        pltpu.VMEM(piece, F32),
        pltpu.VMEM((2 * members * members * 8, picked), F32),
        dma((3,)),
        dma((3,)),
    ]
    for count in (members, members, members, members, 3, members):
        scratch += [dma((count,)), dma((count,))]
    operands = (
        states,
        batch_index,
        obs_pick,
        norm_gain,
        w_in,
        b_in.reshape(1, width),
        params.reshape(depth, 1, features),
        observed,
        noise.reshape(noise.shape[1:]),
        sigma,
    )
    for place, operand in enumerate(operands):
        shape = (depth, features) if place == 6 else operand.shape
        scratch.append(pltpu.VMEM(shape, operand.dtype))
    scratch += [pltpu.VMEM((depth, 1, features), BF16), dma((10,))]
    return pl.pallas_call(
        functools.partial(kernel, members, entries),
        out_shape=jax.ShapeDtypeStruct((depth, features), BF16),
        in_specs=[hbm] * 10,
        out_specs=vmem,
        scratch_shapes=scratch,
        compiler_params=pltpu.CompilerParams(
            collective_id=0, has_side_effects=True, vmem_limit_bytes=63 * 1024 * 1024
        ),
        cost_estimate=pl.CostEstimate(flops=4 * 10**9, bytes_accessed=4 * 10**6, transcendentals=10**6),
    )(*operands).reshape(params.shape)


def hidden_layer(state, norm_gain, w_in, b_in):
    normed = (
        state * lax.rsqrt(jnp.mean(state * state, axis=-1, keepdims=True) + EPS) * norm_gain
    ).astype(jnp.bfloat16)
    return jax.nn.gelu(jnp.dot(normed, w_in, preferred_element_type=jnp.float32) + b_in).astype(
        jnp.bfloat16
    )


def member_sums(pieces):
    weighted, misfit_w = pieces
    count = weighted.shape[0]
    gram_list = []
    innov_list = []
    for item_index in range(weighted.shape[1]):
        flat = weighted[:, item_index].reshape(count, -1).astype(jnp.float32)
        anomaly = (flat - jnp.mean(flat, axis=0)).astype(jnp.bfloat16)
        misfit_flat = misfit_w[:, item_index].reshape(count, -1)
        gram_list.append(
            lax.dot_general(
                anomaly, anomaly, (((1,), (1,)), ((), ())), preferred_element_type=jnp.float32
            )
        )
        innov_list.append(
            lax.dot_general(
                anomaly, misfit_flat, (((1,), (1,)), ((), ())), preferred_element_type=jnp.float32
            )
        )
    return (jnp.stack(gram_list, axis=0), jnp.stack(innov_list, axis=0))


def solve_columns(system, right_side):
    lower_factor = jnp.linalg.cholesky(system)
    halfway = lax.linalg.triangular_solve(lower_factor, right_side, left_side=True, lower=True)
    return lax.linalg.triangular_solve(
        lower_factor, halfway, left_side=True, lower=True, transpose_a=True
    )


def spread_out(
    states,
    batch_index,
    obs_pick,
    norm_gain,
    w_in,
    b_in,
    member_params,
    observed,
    perturbation,
    inv_sigma,
):
    local_members = member_params.shape[0]
    width = w_in.shape[1]
    features = w_in.shape[0]
    step_count = batch_index.shape[0]
    picked = obs_pick.shape[1]
    whole_params = lax.all_gather(member_params, "rep", axis=1, tiled=True)
    weights = whole_params.reshape(local_members, width, features)
    step_scale = DT * width ** (-0.5)
    start_state = jnp.take(states, batch_index, axis=0).astype(jnp.float32)
    shared = hidden_layer(start_state, norm_gain, w_in, b_in)
    current = start_state[None] + step_scale * jnp.einsum(
        "kbh,jhs->jkbs", shared, weights, preferred_element_type=jnp.float32
    )
    layer = hidden_layer(current, norm_gain, w_in, b_in)
    current = current + step_scale * jnp.einsum(
        "jkbh,jhs->jkbs", layer, weights, preferred_element_type=jnp.float32
    )
    feature_ids = lax.broadcasted_iota(jnp.int32, (step_count, features, picked), 1)
    selector = (feature_ids == obs_pick[:, None, :]).astype(jnp.float32)
    predicted = jnp.einsum("jkbs,ksf->jkbf", current, selector, precision=lax.Precision.HIGHEST)
    weighted = (predicted * inv_sigma).astype(jnp.bfloat16)
    misfit_w = (
        observed.astype(jnp.float32) * inv_sigma
        + perturbation.astype(jnp.float32)
        - predicted * inv_sigma
    ).astype(jnp.bfloat16)
    misfit_local = jnp.sum(jnp.square(misfit_w.astype(jnp.float32)))
    gram_items, innov_items = member_sums(
        (
            lax.all_to_all(weighted, "mem", split_axis=2, concat_axis=0, tiled=True),
            lax.all_to_all(misfit_w, "mem", split_axis=2, concat_axis=0, tiled=True),
        )
    )
    gram_matrix = jnp.sum(gram_items, axis=0)
    innovation = jnp.sum(innov_items, axis=0)
    members = gram_matrix.shape[0]
    entries = members * step_count * batch_index.shape[1] * lax.axis_size("rep") * picked
    identity = jnp.eye(members, dtype=jnp.float32)
    gram_matrix, innovation, misfit_total = lax.psum(
        (gram_matrix, innovation, misfit_local), ("mem", "rep")
    )
    system = gram_matrix + (1.0 + misfit_total / entries) * (members - 1) * identity
    coefficients = solve_columns(system, innovation)
    param_block = lax.all_to_all(member_params, "mem", split_axis=1, concat_axis=0, tiled=True)
    params_f = param_block.astype(jnp.float32)
    spread = params_f - jnp.mean(params_f, axis=0)
    change = jnp.einsum("kj,kp->jp", coefficients, spread, precision=lax.Precision.HIGHEST)
    renewed = (params_f + change).astype(jnp.bfloat16)
    return lax.all_to_all(renewed, "mem", split_axis=0, concat_axis=1, tiled=True)


def on_device(states, batch_index, obs_pick, norm_gain, w_in, b_in, member_params, observed, perturbation, inv_sigma):
    args = (states, batch_index, obs_pick, norm_gain, w_in, b_in, member_params, observed, perturbation, inv_sigma)
    members, reps = lax.axis_size("mem"), lax.axis_size("rep")
    if members <= 8 and reps == 4 and member_params.shape[0] == 1:
        entries = members * batch_index.size * reps * obs_pick.shape[1]
        return fused(members, reps, entries, *args)
    return spread_out(*args)


def solution(mesh):
    placed = (
        P("rep", None),
        P(None, "rep"),
        P(),
        P(),
        P(),
        P(),
        P("mem", "rep"),
        P(None, "rep", None),
        P("mem", None, "rep", None),
        P(None, "rep", None),
    )
    return jax.shard_map(
        on_device, mesh=mesh, in_specs=placed, out_specs=P("mem", "rep"), check_vma=False
    )
```
